1024 devices in a mesh: dp: 4 (over y), fsdp: 64 (over z, core), tensor: 4 (over x).
Axes of the slice: x: 4, y: 4, z: 32, core: 2. Of those that a mesh axis runs over, the one named last changes fastest.
Arguments:
- momentum: bfloat16 [4, 14336, 8192], P('dp', 'fsdp', 'tensor'), may hold values from -6 to 6
- gradient: bfloat16 [4, 14336, 8192], P('dp', 'fsdp', 'tensor'), may hold values from -100 to 100, as said below
- basis: float32 [256, 8192], P('fsdp', 'tensor'), may hold values from -0.0625 to 0.0625
Outputs:
- momentum_next: bfloat16 [4, 14336, 8192], P('dp', 'fsdp', 'tensor')
- update: bfloat16 [14336, 8192], P('fsdp', 'tensor')
- basis_next: float32 [256, 8192], P('fsdp', 'tensor')
The draws below stay inside these ranges and needn't reach their ends.
Inputs may be any that keep to these rules, and one draw needn't show every extreme that they name: Row and column scales of each replica's gradient vary.
All inputs are finite; a program needn't handle non-finite values.
Results may differ from the reference program's by a relative error of at most 0.027.
Values may be sent and summed in bfloat16 or wider, within the bound.
No kernel may reach another device: no remote copies, remote signals or barrier semaphores. Data moves between devices by JAX's collectives and lax.ppermute only.
A program may use at most 32 MiB of HBM per device.

```python
import jax
import jax.numpy as jnp
from jax import lax

D = 8192
FF = 14336
RANK = 256
REPLICAS = 4


def draw_gradient(key, part):
    key = jax.random.fold_in(key, 11)
    first, second, third = jax.random.split(key, 3)
    shape = (REPLICAS, FF, D)
    values = jax.random.normal(first, shape, jnp.float32)
    row_reach = 1.15
    values = jnp.clip(values, -6.0, 6.0)
    row_scale = jnp.exp(jax.random.uniform(second, (REPLICAS, FF, 1), jnp.float32, -row_reach, row_reach))
    col_scale = jnp.exp(jax.random.uniform(third, (1, 1, D), jnp.float32, -1.15, 1.15))
    return (values * row_scale * col_scale).astype(jnp.bfloat16)


def level_of(own_key, extent, pieces, low, top_value):
    def one(dim, parts):
        draws = jax.random.uniform(jax.random.fold_in(jax.random.fold_in(own_key, 6), dim), (parts,), jnp.float32, low / len(pieces), top_value / len(pieces))
        return jnp.repeat(jnp.exp(draws), extent[dim] // parts).reshape((-1,) + (1,) * (len(extent) - dim - 1))

    loudness = one(*pieces[0])
    for cut in pieces[1:]:
        loudness = loudness * one(*cut)
    return loudness


def scatter_about(key, shape, spread, limit, cuts=(), dtype=jnp.bfloat16):
    values = spread * jax.random.normal(key, shape, jnp.float32)
    if cuts:
        values = values * level_of(key, shape, cuts, -0.22, 0.18)
    return jnp.clip(values, -limit, limit).astype(dtype)


def setup_inputs(seed: int = 0) -> dict:
    key_list = jax.random.split(jax.random.key(seed), 4)
    momentum = scatter_about(key_list[0], (REPLICAS, FF, D), 1.0, 6.0, ((0, 4), (1, 64), (2, 4)))
    gradient = draw_gradient(jax.random.fold_in(key_list[3], 71), 0)
    basis = scatter_about(key_list[2], (RANK, D), D ** -0.5, 0.0625, ((0, 64), (1, 4)), jnp.float32)
    return {"momentum": momentum, "gradient": gradient, "basis": basis}


epsilon = 1e-06

def reference(momentum, gradient, basis):
    basis_h = basis.astype(jnp.bfloat16)
    buffers = []
    left_full = jnp.zeros((FF, RANK), jnp.float32)
    for replica in range(REPLICAS):
        buffer = momentum[replica].astype(jnp.float32) + gradient[replica].astype(jnp.float32)
        buffers.append(buffer)
        buffer_h = buffer.astype(jnp.bfloat16)
        left_full = left_full + jnp.dot(buffer_h, basis_h.T, preferred_element_type=jnp.float32)
    left_full = left_full / REPLICAS
    left_norms = jnp.sqrt(lax.optimization_barrier(jnp.sum(left_full * left_full, axis=0)) + epsilon)
    left_hat = (left_full / left_norms[None, :]).astype(jnp.bfloat16)
    right_full = jnp.zeros((RANK, D), jnp.float32)
    for replica in range(REPLICAS):
        buffer_h = buffers[replica].astype(jnp.bfloat16)
        right_full = right_full + jnp.dot(left_hat.T, buffer_h, preferred_element_type=jnp.float32)
    right_full = right_full / REPLICAS
    right_h = right_full.astype(jnp.bfloat16)
    right_wide = right_h.astype(jnp.float32)
    right_norms = jnp.sqrt(lax.optimization_barrier(jnp.sum(right_wide * right_wide, axis=1)) + epsilon)
    basis_next = right_wide / right_norms[:, None]
    scale = (FF * D / RANK) ** 0.5
    update = (jnp.dot(left_hat, basis_next.astype(jnp.bfloat16), preferred_element_type=jnp.float32) * scale).astype(jnp.bfloat16)
    feedback = jnp.dot(left_hat, right_h, preferred_element_type=jnp.float32)
    momentum_next = jnp.stack([(buffers[replica] - 0.05 * feedback).astype(jnp.bfloat16) for replica in range(REPLICAS)])
    return (momentum_next, update, basis_next)
```

```python
import jax
import jax.numpy as jnp
from jax import lax
from jax.sharding import Mesh, PartitionSpec as P

D = 8192
FF = 14336
RANK = 256

epsilon = 1e-06
f32 = jnp.float32
bf16 = jnp.bfloat16

NEAR = ("zl", "core")
PLANE = ("dp", "tensor")


def exchange(blocks, axes):
    return lax.all_to_all(blocks, axes, 0, 0, tiled=False)


def gather(block, axes):
    count = lax.axis_size(axes)
    return exchange(jnp.broadcast_to(block[None], (count,) + block.shape), axes)


def pair_lanes(values):
    high = lax.reduce_precision(values, 8, 7)
    low = (values - high).astype(bf16)
    high = high.astype(bf16)
    rows = values.shape[0]
    return jnp.concatenate(
        [jnp.broadcast_to(high[:, None], (rows, 64)), jnp.broadcast_to(low[:, None], (rows, 64))], axis=1
    )


def from_lanes(lanes):
    return lanes[..., 0].astype(f32) + lanes[..., 64].astype(f32)


def body(momentum, gradient, basis):
    replicas = lax.axis_size("dp")
    far = lax.axis_size("zh")
    near = lax.axis_size(NEAR)
    plane = lax.axis_size(PLANE)
    me = lax.axis_index("dp")
    own_rows, width = basis.shape
    part = width // replicas
    rank = own_rows * far * near

    own_basis = lax.dynamic_slice_in_dim(basis, me * part, part, 1).astype(bf16)
    far_basis = gather(own_basis, "zh").reshape(far * own_rows, part)

    def column_block(index):
        first = lax.dynamic_slice_in_dim(momentum[0], index * part, part, 1).astype(f32)
        second = lax.dynamic_slice_in_dim(gradient[0], index * part, part, 1).astype(f32)
        return (first + second).astype(bf16)

    pieces = [
        lax.ppermute(
            column_block((me + k) % replicas), "dp", [(i, (i + k) % replicas) for i in range(replicas)]
        )
        for k in range(1, replicas)
    ]
    far_basis, *pieces = lax.optimization_barrier((far_basis, *pieces))
    basis_h = gather(far_basis, NEAR).reshape(rank, part)
    total = column_block(me).astype(f32)
    for piece in pieces:
        total = total + piece.astype(f32)
    mean_h = (total / replicas).astype(bf16)

    left_term = lax.dot_general(
        basis_h, mean_h, (((1,), (1,)), ((), ())), preferred_element_type=f32
    ).astype(bf16)
    ff = left_term.shape[1]
    left_own = jnp.sum(
        exchange(left_term.reshape(plane, rank // plane, ff), PLANE).astype(f32), axis=0
    )
    left_t = gather(left_own.astype(bf16), PLANE).reshape(rank, ff)
    left_wide = left_t.astype(f32)
    squares = jnp.sum(left_wide * left_wide, axis=1)

    right_term = jnp.dot(left_t, mean_h, preferred_element_type=f32).astype(bf16)
    packed = jnp.concatenate([right_term, pair_lanes(squares)], axis=1)
    packed = exchange(packed.reshape(near, rank // near, part + 128), NEAR)
    right_near = jnp.sum(packed[..., :part].astype(f32), axis=0)
    squares_near = jnp.sum(from_lanes(packed[..., part:]), axis=0)
    packed = jnp.concatenate([right_near.astype(bf16), pair_lanes(squares_near)], axis=1)
    packed = exchange(packed.reshape(far, own_rows, part + 128), "zh")
    right_un = jnp.sum(packed[..., :part].astype(f32), axis=0)
    norms = jnp.sqrt(jnp.sum(from_lanes(packed[..., part:]), axis=0) + epsilon)
    right_own = (right_un / norms[:, None]).astype(bf16)

    packed = jnp.concatenate([right_own, pair_lanes(norms)], axis=1)
    packed = gather(packed, "zh").reshape(far * own_rows, part + 128)
    packed = gather(packed, ("dp",) + NEAR).reshape(replicas, rank, part + 128)
    right_h = packed[..., :part]
    norms_all = from_lanes(packed[0, :, part:])
    left_hat = (left_wide / norms_all[:, None]).astype(bf16)
    right_wide = right_h.astype(f32)
    right_squares = lax.psum(jnp.sum(right_wide * right_wide, axis=(0, 2)), "tensor")
    right_norms = jnp.sqrt(right_squares + epsilon)
    next_h = (right_wide / right_norms[None, :, None]).astype(bf16)

    row = (lax.axis_index(NEAR) * far + lax.axis_index("zh")) * own_rows
    own_right = lax.dynamic_slice_in_dim(right_h, row, own_rows, 1).astype(f32)
    own_norms = lax.dynamic_slice_in_dim(right_norms, row, own_rows, 0)
    basis_next = (own_right / own_norms[None, :, None]).transpose(1, 0, 2).reshape(own_rows, width)

    scale = (FF * D / RANK) ** 0.5
    update, momentum_next = [], []
    for d in range(replicas):
        def product(right):
            return lax.dot_general(
                left_hat, right, (((0,), (0,)), ((), ())), preferred_element_type=f32
            )

        columns = slice(d * part, (d + 1) * part)
        buffer = momentum[0, :, columns].astype(f32) + gradient[0, :, columns].astype(f32)
        momentum_next.append((buffer - 0.05 * product(right_h[d])).astype(bf16))
        update.append((product(next_h[d]) * scale).astype(bf16))
    return (
        jnp.concatenate(momentum_next, axis=1)[None],
        jnp.concatenate(update, axis=1),
        basis_next,
    )


def solution(mesh):
    replicas, fsdp, tensor = (mesh.shape[name] for name in ("dp", "fsdp", "tensor"))
    fine = Mesh(
        mesh.devices.reshape(replicas, fsdp // 4, 2, 2, tensor), ("dp", "zh", "zl", "core", "tensor")
    )
    z = ("zh", "zl", "core")
    return jax.shard_map(
        body,
        mesh=fine,
        in_specs=(P("dp", z, "tensor"), P("dp", z, "tensor"), P(z, "tensor")),
        out_specs=(P("dp", z, "tensor"), P(z, "tensor"), P(z, "tensor")),
        check_vma=False,
    )
```

```python
import functools

import jax
import jax.numpy as jnp
from jax import lax
from jax.experimental import pallas as pl
from jax.experimental.pallas import tpu as pltpu
from jax.sharding import Mesh, PartitionSpec as P

D = 8192
FF = 14336
RANK = 256

epsilon = 1e-06
f32 = jnp.float32
bf16 = jnp.bfloat16

NEAR = ("core", "zl")
LANES = 128


def exchange(blocks, axes, first=0):
    groups = None
    if first:
        count = lax.axis_size(axes)
        groups = [[(i + first) % count for i in range(count)]]
    return lax.all_to_all(blocks, axes, 0, 0, axis_index_groups=groups, tiled=False)


def gather(block, axes, first=0):
    count = lax.axis_size(axes)
    return exchange(jnp.broadcast_to(block[None], (count,) + block.shape), axes, first)


def pair_lanes(values):
    high = lax.reduce_precision(values, 8, 7)
    low = (values - high).astype(bf16)
    high = high.astype(bf16)
    rows = values.shape[0]
    half = (rows, LANES // 2)
    return jnp.concatenate(
        [jnp.broadcast_to(high[:, None], half), jnp.broadcast_to(low[:, None], half)], axis=1
    )


def from_lanes(lanes):
    return lanes[..., 0].astype(f32) + lanes[..., LANES // 2].astype(f32)


def finish_kernel(
    scale, core_ref, left_ref, norms_ref, mine_ref, other_ref, m_ref, g_ref, next_ref, update_ref, lefts, rights
):
    rows = left_ref.shape[0]
    pair, block, part = mine_ref.shape
    core = core_ref[0]

    @pl.when(pl.program_id(0) == 0)
    def _():
        hat = left_ref[...].astype(f32) / norms_ref[0:1]
        lefts[:rows] = hat.astype(bf16)
        lefts[rows:] = (hat / norms_ref[1:2]).astype(bf16)

    rights[core] = mine_ref[...].reshape(pair * block, part)
    rights[1 - core] = other_ref[...].reshape(pair * block, part)
    products = jnp.dot(
        lefts[...], rights[...].reshape(2 * pair * block, part), preferred_element_type=f32
    )
    buffer = m_ref[...].astype(f32) + g_ref[...].astype(f32)
    next_ref[...] = (buffer - 0.05 * products[:rows]).astype(bf16)
    update_ref[...] = (products[rows:] * scale).astype(bf16)


def finish(core, left, norms, mine, other, momentum, gradient, scale):
    replicas, pair, block, _ = mine.shape
    rows, rank = left.shape
    part = mine.shape[3] - LANES
    tile = pl.BlockSpec((rows, part), lambda d: (0, d))
    right = pl.BlockSpec((None, pair, block, part), lambda d: (d, 0, 0, 0))
    wide = jax.ShapeDtypeStruct((rows, replicas * part), bf16)
    return pl.pallas_call(
        functools.partial(finish_kernel, scale),
        grid=(replicas,),
        in_specs=[
            pl.BlockSpec(memory_space=pltpu.SMEM),
            pl.BlockSpec((rows, rank), lambda d: (0, 0)),
            pl.BlockSpec((2, rank), lambda d: (0, 0)),
            right,
            right,
            tile,
            tile,
        ],
        out_specs=[tile, tile],
        out_shape=[wide, wide],
        scratch_shapes=[pltpu.VMEM((2 * rows, rank), bf16), pltpu.VMEM((2, rank // 2, part), bf16)],
        compiler_params=pltpu.CompilerParams(vmem_limit_bytes=24 * 1024 * 1024),
    )(core[None], left, norms, mine, other, momentum, gradient)


def body(momentum, gradient, basis):
    replicas = lax.axis_size("dp")
    far = lax.axis_size("zh")
    near = lax.axis_size(NEAR)
    me = lax.axis_index("dp")
    core = lax.axis_index("core")
    own_rows, width = basis.shape
    part = width // replicas
    rank = own_rows * far * near
    half = rank // 2

    own_basis = lax.dynamic_slice_in_dim(basis, me * part, part, 1).astype(bf16)
    far_basis = gather(own_basis, "zh", far // 2).reshape(far * own_rows, part)

    def column_block(index):
        first = lax.dynamic_slice_in_dim(momentum[0], index * part, part, 1).astype(f32)
        second = lax.dynamic_slice_in_dim(gradient[0], index * part, part, 1).astype(f32)
        return (first + second).astype(bf16)

    pieces = [
        lax.ppermute(
            column_block((me + k) % replicas), "dp", [(i, (i + k) % replicas) for i in range(replicas)]
        )
        for k in range(1, replicas)
    ]
    far_basis, *pieces = lax.optimization_barrier((far_basis, *pieces))
    basis_h = gather(far_basis, NEAR).reshape(rank, part)
    total = column_block(me).astype(f32)
    for piece in pieces:
        total = total + piece.astype(f32)
    mean_h = (total / replicas).astype(bf16)

    left = lax.dot_general(basis_h, mean_h, (((1,), (1,)), ((), ())), preferred_element_type=f32).T
    left = jnp.sum(gather(left.astype(bf16), "tensor").astype(f32), axis=0)
    left = jnp.sum(gather(left.astype(bf16), "dp").astype(f32), axis=0)
    squares = jnp.sum(left * left, axis=0)
    left_h = left.astype(bf16)

    right_term = lax.dot_general(
        left_h, mean_h, (((0,), (0,)), ((), ())), preferred_element_type=f32
    ).astype(bf16)
    packed = jnp.concatenate([right_term, pair_lanes(squares)], axis=1)
    packed = exchange(packed.reshape(near, rank // near, part + LANES), NEAR)
    right_near = jnp.sum(packed[..., :part].astype(f32), axis=0)
    squares_near = jnp.sum(from_lanes(packed[..., part:]), axis=0)
    packed = jnp.concatenate([right_near.astype(bf16), pair_lanes(squares_near)], axis=1)
    packed = exchange(packed.reshape(far, own_rows, part + LANES), "zh")
    right_un = jnp.sum(packed[..., :part].astype(f32), axis=0)
    norms = jnp.sqrt(jnp.sum(from_lanes(packed[..., part:]), axis=0) + epsilon)
    right_own = (right_un / norms[:, None]).astype(bf16)

    packed = jnp.concatenate([right_own, pair_lanes(norms)], axis=1)
    packed = gather(packed, "zh").reshape(far * own_rows, part + LANES)
    packed = gather(packed, ("dp", "zl")).reshape(replicas, 2, half // 2, part + LANES)
    other = lax.ppermute(packed, "core", [(0, 1), (1, 0)])

    right_wide = packed[..., :part].astype(f32)
    right_squares = jnp.sum(right_wide * right_wide, axis=(0, 3)).reshape(1, half)
    left_norms = from_lanes(packed[0, ..., part:]).reshape(1, half)
    both = gather(jnp.concatenate([left_norms, right_squares]), ("core", "tensor"))
    both = both.reshape(2, -1, 2, half)
    right_norms = jnp.sqrt(jnp.sum(both[:, :, 1], axis=1) + epsilon).reshape(rank)
    norms = jnp.stack([both[:, 0, 0].reshape(rank), right_norms])
    momentum_next, update = finish(
        core, left_h, norms, packed, other, momentum[0], gradient[0], (FF * D / RANK) ** 0.5
    )

    place = (lax.axis_index("zh") + far // 2) % far
    pair = lax.axis_index("zl")
    rows = lax.dynamic_slice(
        packed, (0, pair, place * own_rows, 0), (replicas, 1, own_rows, part)
    )[:, 0]
    first = core * half + pair * (half // 2) + place * own_rows
    own_norms = lax.dynamic_slice(right_norms, (first,), (own_rows,))
    basis_next = (
        (rows.astype(f32) / own_norms[None, :, None]).transpose(1, 0, 2).reshape(own_rows, width)
    )
    return (momentum_next[None], update, basis_next)


def solution(mesh):
    replicas, fsdp, tensor = (mesh.shape[name] for name in ("dp", "fsdp", "tensor"))
    fine = Mesh(
        mesh.devices.reshape(replicas, fsdp // 4, 2, 2, tensor), ("dp", "zh", "zl", "core", "tensor")
    )
    z = ("zh", "zl", "core")
    return jax.shard_map(
        body,
        mesh=fine,
        in_specs=(P("dp", z, "tensor"), P("dp", z, "tensor"), P(z, "tensor")),
        out_specs=(P("dp", z, "tensor"), P(z, "tensor"), P(z, "tensor")),
        check_vma=False,
    )
```

```python
import functools

import jax
import jax.numpy as jnp
from jax import lax
from jax.experimental import pallas as pl
from jax.experimental.pallas import tpu as pltpu
from jax.sharding import Mesh, PartitionSpec as P

D = 8192
FF = 14336
RANK = 256

epsilon = 1e-06
f32 = jnp.float32
bf16 = jnp.bfloat16

NEAR = ("core", "zl")
LANES = 128


def exchange(blocks, axes, first=0):
    groups = None
    if first:
        count = lax.axis_size(axes)
        groups = [[(i + first) % count for i in range(count)]]
    return lax.all_to_all(blocks, axes, 0, 0, axis_index_groups=groups, tiled=False)


def gather(block, axes, first=0):
    count = lax.axis_size(axes)
    return exchange(jnp.broadcast_to(block[None], (count,) + block.shape), axes, first)


def pair_lanes(values):
    high = lax.reduce_precision(values, 8, 7)
    low = (values - high).astype(bf16)
    high = high.astype(bf16)
    rows = values.shape[0]
    half = (rows, LANES // 2)
    return jnp.concatenate(
        [jnp.broadcast_to(high[:, None], half), jnp.broadcast_to(low[:, None], half)], axis=1
    )


def from_lanes(lanes):
    return lanes[..., 0].astype(f32) + lanes[..., LANES // 2].astype(f32)


def finish_kernel(
    scale, core_ref, left_ref, norms_ref, mine_ref, other_ref, m_ref, g_ref, own_ref, own_norms_ref,
    next_ref, update_ref, basis_ref, lefts, rights
):
    rows = left_ref.shape[0]
    pair, block, part = mine_ref.shape
    core = core_ref[0]

    @pl.when(pl.program_id(0) == 0)
    def _():
        hat = left_ref[...].astype(f32) / norms_ref[0:1]
        lefts[:rows] = hat.astype(bf16)
        lefts[rows:] = (hat / norms_ref[1:2]).astype(bf16)

    rights[core] = mine_ref[...].reshape(pair * block, part)
    rights[1 - core] = other_ref[...].reshape(pair * block, part)
    products = jnp.dot(
        lefts[...], rights[...].reshape(2 * pair * block, part), preferred_element_type=f32
    )
    buffer = m_ref[...].astype(f32) + g_ref[...].astype(f32)
    next_ref[...] = (buffer - 0.05 * products[:rows]).astype(bf16)
    update_ref[...] = (products[rows:] * scale).astype(bf16)
    basis_ref[...] = own_ref[...].astype(f32) / own_norms_ref[...]


def finish(core, left, norms, mine, other, momentum, gradient, own, own_norms, scale):
    replicas, pair, block, _ = mine.shape
    rows, rank = left.shape
    part = mine.shape[3] - LANES
    tile = pl.BlockSpec((rows, part), lambda d: (0, d))
    right = pl.BlockSpec((None, pair, block, part), lambda d: (d, 0, 0, 0))
    wide = jax.ShapeDtypeStruct((rows, replicas * part), bf16)
    return pl.pallas_call(
        functools.partial(finish_kernel, scale),
        grid=(replicas,),
        in_specs=[
            pl.BlockSpec(memory_space=pltpu.SMEM),
            pl.BlockSpec((rows, rank), lambda d: (0, 0)),
            pl.BlockSpec((2, rank), lambda d: (0, 0)),
            right,
            right,
            tile,
            tile,
            pl.BlockSpec((None, own.shape[1], part), lambda d: (d, 0, 0)),
            pl.BlockSpec(own_norms.shape, lambda d: (0, 0)),
        ],
        out_specs=[tile, tile, pl.BlockSpec((own.shape[1], part), lambda d: (0, d))],
        out_shape=[wide, wide, jax.ShapeDtypeStruct((own.shape[1], replicas * part), f32)],
        scratch_shapes=[pltpu.VMEM((2 * rows, rank), bf16), pltpu.VMEM((2, rank // 2, part), bf16)],
        compiler_params=pltpu.CompilerParams(vmem_limit_bytes=24 * 1024 * 1024),
    )(core[None], left, norms, mine, other, momentum, gradient, own, own_norms)


def body(momentum, gradient, basis):
    replicas = lax.axis_size("dp")
    far = lax.axis_size("zh")
    near = lax.axis_size(NEAR)
    me = lax.axis_index("dp")
    core = lax.axis_index("core")
    own_rows, width = basis.shape
    part = width // replicas
    rank = own_rows * far * near
    half = rank // 2

    own_basis = lax.dynamic_slice_in_dim(basis, me * part, part, 1).astype(bf16)
    far_basis = gather(own_basis, "zh", far // 2).reshape(far * own_rows, part)

    def column_block(index):
        first = lax.dynamic_slice_in_dim(momentum[0], index * part, part, 1).astype(f32)
        second = lax.dynamic_slice_in_dim(gradient[0], index * part, part, 1).astype(f32)
        return (first + second).astype(bf16)

    pieces = [
        lax.ppermute(
            column_block((me + k) % replicas), "dp", [(i, (i + k) % replicas) for i in range(replicas)]
        )
        for k in range(1, replicas)
    ]
    total = column_block(me).astype(f32)
    for piece in pieces:
        total = total + piece.astype(f32)
    mean_h = (total / replicas).astype(bf16)
    far_basis, mean_h = lax.optimization_barrier((far_basis, mean_h))
    basis_h = gather(far_basis, NEAR).reshape(rank, part)

    left = lax.dot_general(basis_h, mean_h, (((1,), (1,)), ((), ())), preferred_element_type=f32).T
    left = jnp.sum(gather(left.astype(bf16), "tensor").astype(f32), axis=0)
    left = jnp.sum(gather(left.astype(bf16), "dp").astype(f32), axis=0)
    squares = jnp.sum(left * left, axis=0)
    left_h = left.astype(bf16)

    right_term = lax.dot_general(
        left_h, mean_h, (((0,), (0,)), ((), ())), preferred_element_type=f32
    ).astype(bf16)
    packed = jnp.concatenate([right_term, pair_lanes(squares)], axis=1)
    packed = exchange(packed.reshape(near, rank // near, part + LANES), NEAR)
    right_near = jnp.sum(packed[..., :part].astype(f32), axis=0)
    squares_near = jnp.sum(from_lanes(packed[..., part:]), axis=0)
    packed = jnp.concatenate([right_near.astype(bf16), pair_lanes(squares_near)], axis=1)
    packed = exchange(packed.reshape(far, own_rows, part + LANES), "zh", far // 8)
    right_un = jnp.sum(packed[..., :part].astype(f32), axis=0)
    norms = jnp.sqrt(jnp.sum(from_lanes(packed[..., part:]), axis=0) + epsilon)
    right_own = (right_un / norms[:, None]).astype(bf16)

    packed = jnp.concatenate([right_own, pair_lanes(norms)], axis=1)
    packed = gather(packed, "zh", far // 8).reshape(far * own_rows, part + LANES)
    packed = gather(packed, ("dp", "zl")).reshape(replicas, 2, half // 2, part + LANES)
    other = lax.ppermute(packed, "core", [(0, 1), (1, 0)])

    right_wide = packed[..., :part].astype(f32)
    right_squares = jnp.sum(right_wide * right_wide, axis=(0, 3)).reshape(1, half)
    left_norms = from_lanes(packed[0, ..., part:]).reshape(1, half)
    both = gather(jnp.concatenate([left_norms, right_squares]), ("core", "tensor"))
    both = both.reshape(2, -1, 2, half)
    right_norms = jnp.sqrt(jnp.sum(both[:, :, 1], axis=1) + epsilon).reshape(rank)
    norms = jnp.stack([both[:, 0, 0].reshape(rank), right_norms])
    place = (lax.axis_index("zh") + far // 2) % far
    pair = lax.axis_index("zl")
    gathered, right_norms = lax.optimization_barrier((packed, right_norms))
    own = lax.dynamic_slice(
        gathered, (0, pair, place * own_rows, 0), (replicas, 1, own_rows, part)
    )[:, 0]
    first = core * half + pair * (half // 2) + place * own_rows
    own_norms = lax.dynamic_slice(right_norms, (first,), (own_rows,))[:, None]
    momentum_next, update, basis_next = finish(
        core, left_h, norms, packed, other, momentum[0], gradient[0], own, own_norms,
        (FF * D / RANK) ** 0.5,
    )
    return (momentum_next[None], update, basis_next)


def solution(mesh):
    replicas, fsdp, tensor = (mesh.shape[name] for name in ("dp", "fsdp", "tensor"))
    fine = Mesh(
        mesh.devices.reshape(replicas, fsdp // 4, 2, 2, tensor), ("dp", "zh", "zl", "core", "tensor")
    )
    z = ("zh", "zl", "core")
    return jax.shard_map(
        body,
        mesh=fine,
        in_specs=(P("dp", z, "tensor"), P("dp", z, "tensor"), P(z, "tensor")),
        out_specs=(P("dp", z, "tensor"), P(z, "tensor"), P(z, "tensor")),
        check_vma=False,
    )
```

```python
import functools

import jax
import jax.numpy as jnp
from jax import lax
from jax.experimental import pallas as pl
from jax.experimental.pallas import tpu as pltpu
from jax.sharding import Mesh, PartitionSpec as P

D = 8192
FF = 14336
RANK = 256

epsilon = 1e-06
f32 = jnp.float32
bf16 = jnp.bfloat16

NEAR = ("core", "zl")
LANES = 128


def exchange(blocks, axes, first=0):
    groups = None
    if first:
        count = lax.axis_size(axes)
        groups = [[(i + first) % count for i in range(count)]]
    return lax.all_to_all(blocks, axes, 0, 0, axis_index_groups=groups, tiled=False)


def gather(block, axes, first=0):
    count = lax.axis_size(axes)
    return exchange(jnp.broadcast_to(block[None], (count,) + block.shape), axes, first)


def pair_lanes(values):
    high = lax.reduce_precision(values, 8, 7)
    low = (values - high).astype(bf16)
    high = high.astype(bf16)
    rows = values.shape[0]
    half = (rows, LANES // 2)
    return jnp.concatenate(
        [jnp.broadcast_to(high[:, None], half), jnp.broadcast_to(low[:, None], half)], axis=1
    )


def from_lanes(lanes):
    return lanes[..., 0].astype(f32) + lanes[..., LANES // 2].astype(f32)


def finish_kernel(
    scale, core_ref, left_ref, norms_ref, mine_ref, other_ref, m_ref, g_ref, own_ref, own_norms_ref,
    next_ref, update_ref, basis_ref, lefts, rights
):
    rows = left_ref.shape[0]
    pair, block, part = mine_ref.shape
    core = core_ref[0]

    @pl.when(pl.program_id(0) == 0)
    def _():
        hat = left_ref[...].astype(f32) / norms_ref[0:1]
        lefts[:rows] = hat.astype(bf16)
        lefts[rows:] = (hat / norms_ref[1:2]).astype(bf16)

    rights[core] = mine_ref[...].reshape(pair * block, part)
    rights[1 - core] = other_ref[...].reshape(pair * block, part)
    products = jnp.dot(
        lefts[...], rights[...].reshape(2 * pair * block, part), preferred_element_type=f32
    )
    buffer = m_ref[...].astype(f32) + g_ref[...].astype(f32)
    next_ref[...] = (buffer - 0.05 * products[:rows]).astype(bf16)
    update_ref[...] = (products[rows:] * scale).astype(bf16)
    basis_ref[...] = own_ref[...].astype(f32) / own_norms_ref[...]


def finish(core, left, norms, mine, other, momentum, gradient, own, own_norms, scale):
    replicas, pair, block, _ = mine.shape
    rows, rank = left.shape
    part = mine.shape[3] - LANES
    tile = pl.BlockSpec((rows, part), lambda d: (0, d))
    right = pl.BlockSpec((None, pair, block, part), lambda d: (d, 0, 0, 0))
    wide = jax.ShapeDtypeStruct((rows, replicas * part), bf16)
    return pl.pallas_call(
        functools.partial(finish_kernel, scale),
        grid=(replicas,),
        in_specs=[
            pl.BlockSpec(memory_space=pltpu.SMEM),
            pl.BlockSpec((rows, rank), lambda d: (0, 0)),
            pl.BlockSpec((2, rank), lambda d: (0, 0)),
            right,
            right,
            tile,
            tile,
            pl.BlockSpec((None, own.shape[1], part), lambda d: (d, 0, 0)),
            pl.BlockSpec(own_norms.shape, lambda d: (0, 0)),
        ],
        out_specs=[tile, tile, pl.BlockSpec((own.shape[1], part), lambda d: (0, d))],
        out_shape=[wide, wide, jax.ShapeDtypeStruct((own.shape[1], replicas * part), f32)],
        scratch_shapes=[pltpu.VMEM((2 * rows, rank), bf16), pltpu.VMEM((2, rank // 2, part), bf16)],
        compiler_params=pltpu.CompilerParams(vmem_limit_bytes=24 * 1024 * 1024),
    )(core[None], left, norms, mine, other, momentum, gradient, own, own_norms)


def body(momentum, gradient, basis):
    replicas = lax.axis_size("dp")
    far = lax.axis_size("zh")
    near = lax.axis_size(NEAR)
    me = lax.axis_index("dp")
    core = lax.axis_index("core")
    own_rows, width = basis.shape
    part = width // replicas
    rank = own_rows * far * near
    half = rank // 2
    early, late = 11 * far // 16, 5 * far // 16

    own_basis = lax.dynamic_slice_in_dim(basis, me * part, part, 1).astype(bf16)
    far_basis = gather(own_basis, "zh", early).reshape(far * own_rows, part)

    def column_block(index):
        first = lax.dynamic_slice_in_dim(momentum[0], index * part, part, 1).astype(f32)
        second = lax.dynamic_slice_in_dim(gradient[0], index * part, part, 1).astype(f32)
        return (first + second).astype(bf16)

    pieces = [
        lax.ppermute(
            column_block((me + k) % replicas), "dp", [(i, (i + k) % replicas) for i in range(replicas)]
        )
        for k in range(1, replicas)
    ]
    total = column_block(me).astype(f32)
    for piece in pieces:
        total = total + piece.astype(f32)
    mean_h = (total / replicas).astype(bf16)
    far_basis, mean_h = lax.optimization_barrier((far_basis, mean_h))
    basis_h = gather(far_basis, NEAR).reshape(rank, part)

    left = lax.dot_general(basis_h, mean_h, (((1,), (1,)), ((), ())), preferred_element_type=f32).T
    left = jnp.sum(gather(left.astype(bf16), "tensor").astype(f32), axis=0)
    left = jnp.sum(gather(left.astype(bf16), "dp").astype(f32), axis=0)
    squares = jnp.sum(left * left, axis=0)
    left_h = left.astype(bf16)

    right_term = lax.dot_general(
        left_h, mean_h, (((0,), (0,)), ((), ())), preferred_element_type=f32
    ).astype(bf16)
    packed = jnp.concatenate([right_term, pair_lanes(squares)], axis=1)
    packed = exchange(packed.reshape(near, rank // near, part + LANES), NEAR)
    right_near = jnp.sum(packed[..., :part].astype(f32), axis=0)
    squares_near = jnp.sum(from_lanes(packed[..., part:]), axis=0)
    packed = jnp.concatenate([right_near.astype(bf16), pair_lanes(squares_near)], axis=1)
    packed = exchange(packed.reshape(far, own_rows, part + LANES), "zh", late)
    right_un = jnp.sum(packed[..., :part].astype(f32), axis=0)
    norms = jnp.sqrt(jnp.sum(from_lanes(packed[..., part:]), axis=0) + epsilon)
    right_own = (right_un / norms[:, None]).astype(bf16)

    packed = jnp.concatenate([right_own, pair_lanes(norms)], axis=1)
    packed = gather(packed, "zh", late).reshape(far * own_rows, part + LANES)
    packed = gather(packed, ("dp", "zl")).reshape(replicas, 2, half // 2, part + LANES)
    other = lax.ppermute(packed, "core", [(0, 1), (1, 0)])

    right_wide = packed[..., :part].astype(f32)
    right_squares = jnp.sum(right_wide * right_wide, axis=(0, 3)).reshape(1, half)
    left_norms = from_lanes(packed[0, ..., part:]).reshape(1, half)
    both = gather(jnp.concatenate([left_norms, right_squares]), ("core", "tensor"))
    both = both.reshape(2, -1, 2, half)
    right_norms = jnp.sqrt(jnp.sum(both[:, :, 1], axis=1) + epsilon).reshape(rank)
    norms = jnp.stack([both[:, 0, 0].reshape(rank), right_norms])
    place = (lax.axis_index("zh") + far - early) % far
    pair = lax.axis_index("zl")
    gathered, right_norms = lax.optimization_barrier((packed, right_norms))
    own = lax.dynamic_slice(
        gathered, (0, pair, place * own_rows, 0), (replicas, 1, own_rows, part)
    )[:, 0]
    first = core * half + pair * (half // 2) + place * own_rows
    own_norms = lax.dynamic_slice(right_norms, (first,), (own_rows,))[:, None]
    momentum_next, update, basis_next = finish(
        core, left_h, norms, packed, other, momentum[0], gradient[0], own, own_norms,
        (FF * D / RANK) ** 0.5,
    )
    return (momentum_next[None], update, basis_next)


def solution(mesh):
    replicas, fsdp, tensor = (mesh.shape[name] for name in ("dp", "fsdp", "tensor"))
    fine = Mesh(
        mesh.devices.reshape(replicas, fsdp // 4, 2, 2, tensor), ("dp", "zh", "zl", "core", "tensor")
    )
    z = ("zh", "zl", "core")
    return jax.shard_map(
        body,
        mesh=fine,
        in_specs=(P("dp", z, "tensor"), P("dp", z, "tensor"), P(z, "tensor")),
        out_specs=(P("dp", z, "tensor"), P(z, "tensor"), P(z, "tensor")),
        check_vma=False,
    )
```

```python
import functools

import jax
import jax.numpy as jnp
from jax import lax
from jax.experimental import pallas as pl
from jax.experimental.pallas import tpu as pltpu
from jax.sharding import Mesh, PartitionSpec as P

D = 8192
FF = 14336
RANK = 256

epsilon = 1e-06
f32 = jnp.float32
bf16 = jnp.bfloat16

NEAR = ("core", "zl")
LANES = 128


def exchange(blocks, axes, first=0):
    groups = None
    if first:
        count = lax.axis_size(axes)
        groups = [[(i + first) % count for i in range(count)]]
    return lax.all_to_all(blocks, axes, 0, 0, axis_index_groups=groups, tiled=False)


def gather(block, axes, first=0):
    count = lax.axis_size(axes)
    return exchange(jnp.broadcast_to(block[None], (count,) + block.shape), axes, first)


def split_rows(values):
    high = lax.reduce_precision(values, 8, 7)
    return jnp.concatenate([high, values - high]).astype(bf16).reshape(-1, LANES)


def joined(rows):
    total = jnp.sum(rows.astype(f32), axis=0)
    half = total.shape[0] // 2
    return (total[:half] + total[half:]).reshape(-1)


def finish_kernel(
    scale, core_ref, left_ref, norms_ref, mine_ref, other_ref, m_ref, g_ref, own_ref, own_norms_ref,
    next_ref, update_ref, basis_ref, lefts, rights
):
    rows = left_ref.shape[0]
    pair, block, part = mine_ref.shape
    core = core_ref[0]

    @pl.when(pl.program_id(0) == 0)
    def _():
        hat = left_ref[...].astype(f32) / norms_ref[0:1]
        lefts[:rows] = hat.astype(bf16)
        lefts[rows:] = (hat / norms_ref[1:2]).astype(bf16)

    rights[core] = mine_ref[...].reshape(pair * block, part)
    rights[1 - core] = other_ref[...].reshape(pair * block, part)
    products = jnp.dot(
        lefts[...], rights[...].reshape(2 * pair * block, part), preferred_element_type=f32
    )
    buffer = m_ref[...].astype(f32) + g_ref[...].astype(f32)
    next_ref[...] = (buffer - 0.05 * products[:rows]).astype(bf16)
    update_ref[...] = (products[rows:] * scale).astype(bf16)
    basis_ref[...] = own_ref[...].astype(f32) / own_norms_ref[...]


def finish(core, left, norms, mine, other, momentum, gradient, own, own_norms, scale):
    replicas, pair, block, _ = mine.shape
    rows, rank = left.shape
    part = mine.shape[3]
    tile = pl.BlockSpec((rows, part), lambda d: (0, d))
    right = pl.BlockSpec((None, pair, block, part), lambda d: (d, 0, 0, 0))
    wide = jax.ShapeDtypeStruct((rows, replicas * part), bf16)
    return pl.pallas_call(
        functools.partial(finish_kernel, scale),
        grid=(replicas,),
        in_specs=[
            pl.BlockSpec(memory_space=pltpu.SMEM),
            pl.BlockSpec((rows, rank), lambda d: (0, 0)),
            pl.BlockSpec((2, rank), lambda d: (0, 0)),
            right,
            right,
            tile,
            tile,
            pl.BlockSpec((None, own.shape[1], part), lambda d: (d, 0, 0)),
            pl.BlockSpec(own_norms.shape, lambda d: (0, 0)),
        ],
        out_specs=[tile, tile, pl.BlockSpec((own.shape[1], part), lambda d: (0, d))],
        out_shape=[wide, wide, jax.ShapeDtypeStruct((own.shape[1], replicas * part), f32)],
        scratch_shapes=[pltpu.VMEM((2 * rows, rank), bf16), pltpu.VMEM((2, rank // 2, part), bf16)],
        compiler_params=pltpu.CompilerParams(vmem_limit_bytes=24 * 1024 * 1024),
    )(core[None], left, norms, mine, other, momentum, gradient, own, own_norms)


def body(momentum, gradient, basis):
    replicas = lax.axis_size("dp")
    far = lax.axis_size("zh")
    near = lax.axis_size(NEAR)
    me = lax.axis_index("dp")
    core = lax.axis_index("core")
    own_rows, width = basis.shape
    part = width // replicas
    rank = own_rows * far * near
    half = rank // 2
    early, late = 11 * far // 16, 5 * far // 16

    own_basis = lax.dynamic_slice_in_dim(basis, me * part, part, 1).astype(bf16)
    far_basis = gather(own_basis, "zh", early).reshape(far * own_rows, part)

    def column_block(index):
        first = lax.dynamic_slice_in_dim(momentum[0], index * part, part, 1).astype(f32)
        second = lax.dynamic_slice_in_dim(gradient[0], index * part, part, 1).astype(f32)
        return (first + second).astype(bf16)

    pieces = [
        lax.ppermute(
            column_block((me + k) % replicas), "dp", [(i, (i + k) % replicas) for i in range(replicas)]
        )
        for k in range(1, replicas)
    ]
    total = column_block(me).astype(f32)
    for piece in pieces:
        total = total + piece.astype(f32)
    mean_h = (total / replicas).astype(bf16)
    zh, pair = lax.axis_index("zh"), lax.axis_index("zl")
    summed = (lax.axis_index(NEAR) * far + (zh + far - late) % far) * own_rows
    place = (zh + far - early) % far * own_rows
    first = core * half + pair * (half // 2) + place
    indices = [index.astype(jnp.uint32) for index in (summed, place, first, pair)]
    far_basis, mean_h, *indices = lax.optimization_barrier((far_basis, mean_h, *indices))
    summed, place, first, pair = indices
    zero = jnp.uint32(0)
    basis_h = gather(far_basis, NEAR).reshape(rank, part)

    left = lax.dot_general(basis_h, mean_h, (((1,), (1,)), ((), ())), preferred_element_type=f32).T
    left = jnp.sum(gather(left.astype(bf16), "tensor").astype(f32), axis=0)
    left = jnp.sum(gather(left.astype(bf16), "dp").astype(f32), axis=0)
    squares = jnp.sum(left * left, axis=0)
    left_h = left.astype(bf16)

    right_term = lax.dot_general(
        left_h, mean_h, (((0,), (0,)), ((), ())), preferred_element_type=f32
    ).astype(bf16)
    def with_squares(right, values):
        lanes = jnp.tile(split_rows(values), (right.shape[0] // own_rows, 1))
        return jnp.concatenate([right, lanes], axis=1)

    packed = with_squares(right_term, squares)
    packed = exchange(packed.reshape(near, rank // near, part + LANES), NEAR)
    right_near = jnp.sum(packed[..., :part].astype(f32), axis=0)
    packed = with_squares(right_near.astype(bf16), joined(packed[:, :own_rows, part:]))
    packed = exchange(packed.reshape(far, own_rows, part + LANES), "zh", late)
    right_un = jnp.sum(packed[..., :part].astype(f32), axis=0)
    left_norms = jnp.sqrt(joined(packed[..., part:]) + epsilon)
    norms = lax.dynamic_slice(left_norms, (summed,), (own_rows,))
    right_own = (right_un / norms[:, None]).astype(bf16)

    packed = gather(right_own, "zh", late).reshape(far * own_rows, part)
    packed = gather(packed, ("dp", "zl")).reshape(replicas, 2, half // 2, part)
    other = lax.ppermute(packed, "core", [(0, 1), (1, 0)])

    right_wide = packed.astype(f32)
    right_squares = jnp.sum(right_wide * right_wide, axis=(0, 3)).reshape(1, half)
    right_squares = gather(right_squares, ("core", "tensor")).reshape(2, -1, half)
    right_norms = jnp.sqrt(jnp.sum(right_squares, axis=1) + epsilon).reshape(rank)
    norms = jnp.stack([left_norms, right_norms])

    gathered, right_norms = lax.optimization_barrier((packed, right_norms))
    own = lax.dynamic_slice(
        gathered, (zero, pair, place, zero), (replicas, 1, own_rows, part)
    )[:, 0]
    own_norms = lax.dynamic_slice(right_norms, (first,), (own_rows,))[:, None]
    momentum_next, update, basis_next = finish(
        core, left_h, norms, packed, other, momentum[0], gradient[0], own, own_norms,
        (FF * D / RANK) ** 0.5,
    )
    return (momentum_next[None], update, basis_next)


def solution(mesh):
    replicas, fsdp, tensor = (mesh.shape[name] for name in ("dp", "fsdp", "tensor"))
    fine = Mesh(
        mesh.devices.reshape(replicas, fsdp // 4, 2, 2, tensor), ("dp", "zh", "zl", "core", "tensor")
    )
    z = ("zh", "zl", "core")
    return jax.shard_map(
        body,
        mesh=fine,
        in_specs=(P("dp", z, "tensor"), P("dp", z, "tensor"), P(z, "tensor")),
        out_specs=(P("dp", z, "tensor"), P(z, "tensor"), P(z, "tensor")),
        check_vma=False,
    )
```

```python
import functools

import jax
import jax.numpy as jnp
from jax import lax
from jax.experimental import pallas as pl
from jax.experimental.pallas import tpu as pltpu
from jax.sharding import Mesh, PartitionSpec as P

D = 8192
FF = 14336
RANK = 256

epsilon = 1e-06
f32 = jnp.float32
bf16 = jnp.bfloat16

NEAR = ("core", "zl")
LANES = 128


def exchange(blocks, axes, first=0):
    groups = None
    if first:
        count = lax.axis_size(axes)
        groups = [[(i + first) % count for i in range(count)]]
    return lax.all_to_all(blocks, axes, 0, 0, axis_index_groups=groups, tiled=False)


def gather(block, axes, first=0):
    count = lax.axis_size(axes)
    return exchange(jnp.broadcast_to(block[None], (count,) + block.shape), axes, first)


def split_rows(values):
    high = lax.reduce_precision(values, 8, 7)
    return jnp.concatenate([high, values - high]).astype(bf16).reshape(-1, LANES)


def joined(rows):
    total = jnp.sum(rows.astype(f32), axis=0)
    half = total.shape[0] // 2
    return (total[:half] + total[half:]).reshape(-1)


def finish_kernel(
    scale, core_ref, left_ref, norms_ref, mine_ref, other_ref, m_ref, g_ref, own_ref, own_norms_ref,
    next_ref, update_ref, basis_ref, lefts, rights
):
    rows = left_ref.shape[0]
    pair, block, part = mine_ref.shape
    core = core_ref[0]

    @pl.when(pl.program_id(0) == 0)
    def _():
        hat = left_ref[...].astype(f32) / norms_ref[0:1]
        lefts[:rows] = hat.astype(bf16)
        lefts[rows:] = (hat / norms_ref[1:2]).astype(bf16)

    rights[core] = mine_ref[...].reshape(pair * block, part)
    rights[1 - core] = other_ref[...].reshape(pair * block, part)
    products = jnp.dot(
        lefts[...], rights[...].reshape(2 * pair * block, part), preferred_element_type=f32
    )
    buffer = m_ref[...].astype(f32) + g_ref[...].astype(f32)
    next_ref[...] = (buffer - 0.05 * products[:rows]).astype(bf16)
    update_ref[...] = (products[rows:] * scale).astype(bf16)
    basis_ref[...] = own_ref[...].astype(f32) / own_norms_ref[...]


def finish(core, left, norms, mine, other, momentum, gradient, own, own_norms, scale):
    replicas, pair, block, _ = mine.shape
    rows, rank = left.shape
    part = mine.shape[3]
    tile = pl.BlockSpec((rows, part), lambda d: (0, d))
    right = pl.BlockSpec((None, pair, block, part), lambda d: (d, 0, 0, 0))
    wide = jax.ShapeDtypeStruct((rows, replicas * part), bf16)
    return pl.pallas_call(
        functools.partial(finish_kernel, scale),
        grid=(replicas,),
        in_specs=[
            pl.BlockSpec(memory_space=pltpu.SMEM),
            pl.BlockSpec((rows, rank), lambda d: (0, 0)),
            pl.BlockSpec((2, rank), lambda d: (0, 0)),
            right,
            right,
            tile,
            tile,
            pl.BlockSpec((None, own.shape[1], part), lambda d: (d, 0, 0)),
            pl.BlockSpec(own_norms.shape, lambda d: (0, 0)),
        ],
        out_specs=[tile, tile, pl.BlockSpec((own.shape[1], part), lambda d: (0, d))],
        out_shape=[wide, wide, jax.ShapeDtypeStruct((own.shape[1], replicas * part), f32)],
        scratch_shapes=[pltpu.VMEM((2 * rows, rank), bf16), pltpu.VMEM((2, rank // 2, part), bf16)],
        compiler_params=pltpu.CompilerParams(vmem_limit_bytes=24 * 1024 * 1024),
    )(core[None], left, norms, mine, other, momentum, gradient, own, own_norms)


def body(momentum, gradient, basis):
    replicas = lax.axis_size("dp")
    far = lax.axis_size("zh")
    near = lax.axis_size(NEAR)
    me = lax.axis_index("dp")
    core = lax.axis_index("core")
    own_rows, width = basis.shape
    part = width // replicas
    rank = own_rows * far * near
    half = rank // 2
    early, late = 11 * far // 16, 5 * far // 16

    own_basis = lax.dynamic_slice_in_dim(basis, me * part, part, 1).astype(bf16)
    far_basis = gather(own_basis, "zh", early).reshape(far * own_rows, part)

    def column_block(index):
        first = lax.dynamic_slice_in_dim(momentum[0], index * part, part, 1).astype(f32)
        second = lax.dynamic_slice_in_dim(gradient[0], index * part, part, 1).astype(f32)
        return (first + second).astype(bf16)

    pieces = [
        lax.ppermute(
            column_block((me + k) % replicas), "dp", [(i, (i + k) % replicas) for i in range(replicas)]
        )
        for k in range(1, replicas)
    ]
    total = column_block(me).astype(f32)
    for piece in pieces:
        total = total + piece.astype(f32)
    mean_h = (total / replicas).astype(bf16)
    zh, pair = lax.axis_index("zh"), lax.axis_index("zl")
    summed = (lax.axis_index(NEAR) * far + (zh + far - late) % far) * own_rows
    place = (zh + far - early) % far * own_rows
    first = core * half + pair * (half // 2) + place
    indices = [index.astype(jnp.uint32) for index in (summed, place, first, pair)]
    far_basis, mean_h, *indices = lax.optimization_barrier((far_basis, mean_h, *indices))
    summed, place, first, pair = indices
    zero = jnp.uint32(0)
    basis_h = gather(far_basis, NEAR).reshape(rank, part)

    left = lax.dot_general(basis_h, mean_h, (((1,), (1,)), ((), ())), preferred_element_type=f32).T
    left = jnp.sum(gather(left.astype(bf16), "dp").astype(f32), axis=0)
    left = jnp.sum(gather(left.astype(bf16), "tensor").astype(f32), axis=0)
    squares = jnp.sum(left * left, axis=0)
    left_h = left.astype(bf16)

    right_term = lax.dot_general(
        left_h, mean_h, (((0,), (0,)), ((), ())), preferred_element_type=f32
    ).astype(bf16)
    def with_squares(right, values):
        lanes = jnp.tile(split_rows(values), (right.shape[0] // own_rows, 1))
        return jnp.concatenate([right, lanes], axis=1)

    packed = with_squares(right_term, squares)
    packed = exchange(packed.reshape(near, rank // near, part + LANES), NEAR)
    right_near = jnp.sum(packed[..., :part].astype(f32), axis=0)
    packed = with_squares(right_near.astype(bf16), joined(packed[:, :own_rows, part:]))
    packed = exchange(packed.reshape(far, own_rows, part + LANES), "zh", late)
    right_un = jnp.sum(packed[..., :part].astype(f32), axis=0)
    left_norms = jnp.sqrt(joined(packed[..., part:]) + epsilon)
    norms = lax.dynamic_slice(left_norms, (summed,), (own_rows,))
    right_own = (right_un / norms[:, None]).astype(bf16)

    packed = gather(right_own, "zh", late).reshape(far * own_rows, part)
    packed = gather(packed, ("dp", "zl")).reshape(replicas, 2, half // 2, part)
    other = lax.ppermute(packed, "core", [(0, 1), (1, 0)])

    right_wide = packed.astype(f32)
    right_squares = jnp.sum(right_wide * right_wide, axis=(0, 3)).reshape(1, half)
    right_squares = gather(right_squares, ("core", "tensor")).reshape(2, -1, half)
    right_norms = jnp.sqrt(jnp.sum(right_squares, axis=1) + epsilon).reshape(rank)
    norms = jnp.stack([left_norms, right_norms])

    gathered, right_norms = lax.optimization_barrier((packed, right_norms))
    own = lax.dynamic_slice(
        gathered, (zero, pair, place, zero), (replicas, 1, own_rows, part)
    )[:, 0]
    own_norms = lax.dynamic_slice(right_norms, (first,), (own_rows,))[:, None]
    momentum_next, update, basis_next = finish(
        core, left_h, norms, packed, other, momentum[0], gradient[0], own, own_norms,
        (FF * D / RANK) ** 0.5,
    )
    return (momentum_next[None], update, basis_next)


def solution(mesh):
    replicas, fsdp, tensor = (mesh.shape[name] for name in ("dp", "fsdp", "tensor"))
    fine = Mesh(
        mesh.devices.reshape(replicas, fsdp // 4, 2, 2, tensor), ("dp", "zh", "zl", "core", "tensor")
    )
    z = ("zh", "zl", "core")
    return jax.shard_map(
        body,
        mesh=fine,
        in_specs=(P("dp", z, "tensor"), P("dp", z, "tensor"), P(z, "tensor")),
        out_specs=(P("dp", z, "tensor"), P(z, "tensor"), P(z, "tensor")),
        check_vma=False,
    )
```
